256 devices in a mesh: kv: 32 (over x, y, core), dp: 8 (over z).
Axes of the slice: x: 4, y: 4, z: 8, core: 2. Of those that a mesh axis runs over, the one named last changes fastest.
Arguments:
- queries: bfloat16 [64, 128, 576], P('dp'), may hold values from -48 to 48
- drafts: bfloat16 [64, 576], P('dp'), may hold values from -18 to 18
- cache: bfloat16 [16, 131072, 576], P('dp', 'kv'), may hold values from -4 to 4
- lengths: int32 [16], P('dp'), may hold values from 65536 to 131072, as said below
- row_seq: int32 [64], P('dp'), may hold values from 0 to 1, as said below
- row_pos: int32 [64], P('dp'), may hold values from 65536 to 131075, as said below
- w_uv: bfloat16 [128, 512, 128], P('kv'), may hold values from -0.25 to 0.25
- w_out: bfloat16 [16384, 7168], P('kv', 'dp'), may hold values from -0.046875 to 0.046875
- hidden: bfloat16 [64, 7168], P(None, 'dp'), may hold values from -0.59765625 to 0.59765625
- gain: float32 [7168], P('dp'), may hold values from 0.1 to 1.9
- w_gate: bfloat16 [7168, 18432], P('dp', 'kv'), may hold values from -0.0625 to 0.0625
- w_up: bfloat16 [7168, 18432], P('dp', 'kv'), may hold values from -0.0625 to 0.0625
- w_down: bfloat16 [18432, 7168], P('kv', 'dp'), may hold values from -0.01171875 to 0.01171875
Outputs:
- mixed: bfloat16 [64, 7168], P(None, 'dp')
The draws below stay inside these ranges and needn't reach their ends.
Inputs may be any that keep to these rules, and one draw needn't show every extreme that they name: `lengths`: sequence 0 has exactly 131072 live positions. `row_seq`: each of a group's 2 sequences owns exactly 4 rows of the group, in any order. `row_pos`: A row's position is its sequence's length plus a step number; the 4 rows of one sequence take the step numbers 0 to 3 once each.
All inputs are finite; a program needn't handle non-finite values.
Results may differ from the reference program's by a relative error of at most 0.009.
Values may be sent and summed in bfloat16 or wider, within the bound.
A program may use at most 128 MiB of HBM per device.

```python
import jax
import jax.numpy as jnp
from jax import lax

D = 7168
H = 128
LAT = 512
ROPE = 64
HD = 128
FF = 18432
SEQ_DP = 2
STEPS = 4
CTX = 131072
TOKENS = 64
N_DP = 8


def layout(key):
    keys_all = jax.random.split(key, 5)
    seq_total = SEQ_DP * N_DP
    tok_group = SEQ_DP * STEPS
    lengths = jax.random.randint(keys_all[0], (seq_total,), CTX // 2, CTX + 1).at[0].set(CTX)
    orders = jax.vmap(lambda sub: jax.random.permutation(sub, tok_group))(jax.random.split(keys_all[1], N_DP))
    seq_local = orders // STEPS
    step_num = orders % STEPS
    seq_global = jnp.arange(N_DP)[:, None] * SEQ_DP + seq_local
    positions = lengths[seq_global] + step_num
    offsets = jax.random.randint(keys_all[2], (seq_total,), 0, CTX // (4 * STEPS))
    spots = 2 * step_num + 2 * STEPS * offsets[seq_global]
    aligned = jnp.clip(jax.random.normal(keys_all[3], (tok_group * N_DP, LAT + ROPE)), -4.0, 4.0)
    aligned = aligned.astype(jnp.bfloat16).astype(jnp.float32)
    return (lengths, seq_local.reshape(-1), positions.reshape(-1), seq_global.reshape(-1), spots.reshape(-1), aligned, keys_all[4])


def draw_lengths(key, part):
    shared = layout(key)
    return shared[0].astype(jnp.int32)


def draw_row_seq(key, part):
    shared = layout(key)
    return shared[1].astype(jnp.int32)


def draw_row_pos(key, part):
    shared = layout(key)
    return shared[2].astype(jnp.int32)


def draw_cache(key, part):
    key = jax.random.fold_in(key, 11)
    base = jnp.clip(jax.random.normal(key, (SEQ_DP * N_DP, CTX, LAT + ROPE)), -4.0, 4.0)
    return base.astype(jnp.bfloat16)


def draw_queries(key, part):
    key = jax.random.fold_in(key, 13)
    row_total = SEQ_DP * STEPS * N_DP
    base = jnp.clip(1.5 * jax.random.normal(key, (row_total, H, LAT + ROPE)), -9.0, 9.0)
    return base.astype(jnp.bfloat16)


def shard_levels(stream_key, shape, cuts, low, top_value):
    level = 1.0
    for axis_at, shards_of in cuts:
        heights = jax.random.uniform(jax.random.fold_in(jax.random.fold_in(stream_key, 6), axis_at), (shards_of,), jnp.float32, low / len(cuts), top_value / len(cuts))
        level = level * jnp.repeat(jnp.exp(heights), shape[axis_at] // shards_of).reshape((-1,) + (1,) * (len(shape) - 1 - axis_at))
    return level


def gaussian(rng, extent, width, most, cuts=(), kind=jnp.bfloat16):
    entries = jax.random.normal(rng, extent, jnp.float32) * width
    if len(cuts) > 0:
        entries = shard_levels(rng, extent, cuts, -0.22, 0.18) * entries
    return jnp.clip(entries, min=-most, max=most).astype(kind)


def setup_inputs(seed: int = 0) -> dict:
    arg_keys = jax.random.split(jax.random.key(seed), 14)
    return {
        "queries": draw_queries(jax.random.fold_in(arg_keys[13], 71), 0),
        "drafts": gaussian(arg_keys[1], (TOKENS, LAT + ROPE), 3.0, 18.0, ((0, 8),)),
        "cache": draw_cache(jax.random.fold_in(arg_keys[13], 71), 0),
        "lengths": draw_lengths(jax.random.fold_in(arg_keys[13], 71), 0),
        "row_seq": draw_row_seq(jax.random.fold_in(arg_keys[13], 71), 0),
        "row_pos": draw_row_pos(jax.random.fold_in(arg_keys[13], 71), 0),
        "w_uv": gaussian(arg_keys[6], (H, LAT, HD), LAT ** -0.5, 0.25, ((0, 32),)),
        "w_out": gaussian(arg_keys[7], (H * HD, D), (H * HD) ** -0.5, 0.046875, ((0, 32), (1, 8))),
        "hidden": gaussian(arg_keys[8], (TOKENS, D), 0.1, 0.59765625, ((1, 8),)),
        "gain": jnp.clip(1.0 + 0.18 * jax.random.normal(arg_keys[9], (D,), jnp.float32), 0.1, 1.9),
        "w_gate": gaussian(arg_keys[10], (D, FF), D ** -0.5, 0.0625, ((0, 8), (1, 32))),
        "w_up": gaussian(arg_keys[11], (D, FF), D ** -0.5, 0.0625, ((0, 8), (1, 32))),
        "w_down": gaussian(arg_keys[12], (FF, D), (16 * FF) ** -0.5, 0.01171875, ((0, 32), (1, 8))),
    }


def attend_row(token, queries, drafts, cache, lengths, row_seq, row_pos):
    tok_group = SEQ_DP * STEPS
    group = token // tok_group
    seq_local = row_seq[token]
    seq_global = (group * SEQ_DP + seq_local).astype(jnp.int32)
    key_rows = lax.dynamic_index_in_dim(cache, seq_global, 0, keepdims=False)
    query = queries[token]
    qk_scale = (HD + ROPE) ** (-0.5)
    cache_scores = jnp.dot(query, key_rows.T, preferred_element_type=jnp.float32) * qk_scale
    cache_valid = jnp.arange(CTX, dtype=jnp.int32) < lengths[seq_global]
    group_start = (group * tok_group).astype(jnp.int32)
    draft_rows = lax.dynamic_slice_in_dim(drafts, group_start, tok_group, 0)
    draft_seq = lax.dynamic_slice_in_dim(row_seq, group_start, tok_group, 0)
    draft_pos = lax.dynamic_slice_in_dim(row_pos, group_start, tok_group, 0)
    draft_valid = (draft_seq == seq_local) & (draft_pos <= row_pos[token])
    draft_scores = jnp.dot(query, draft_rows.T, preferred_element_type=jnp.float32) * qk_scale
    lowest = -jnp.inf
    peak = jnp.maximum(lax.optimization_barrier(jnp.max(jnp.where(cache_valid[None, :], cache_scores, lowest), axis=1)), lax.optimization_barrier(jnp.max(jnp.where(draft_valid[None, :], draft_scores, lowest), axis=1)))
    cache_weight = jnp.where(cache_valid[None, :], jnp.exp(cache_scores - peak[:, None]), 0.0)
    draft_weight = jnp.where(draft_valid[None, :], jnp.exp(draft_scores - peak[:, None]), 0.0)
    denom = lax.optimization_barrier(jnp.sum(cache_weight, axis=1)) + lax.optimization_barrier(jnp.sum(draft_weight, axis=1))
    numer = jnp.dot(cache_weight.astype(jnp.bfloat16), key_rows[:, :LAT], preferred_element_type=jnp.float32)
    numer = numer + jnp.dot(draft_weight.astype(jnp.bfloat16), draft_rows[:, :LAT], preferred_element_type=jnp.float32)
    return (numer / denom[:, None]).astype(jnp.bfloat16)

def reference(queries, drafts, cache, lengths, row_seq, row_pos, w_uv, w_out, hidden, gain, w_gate, w_up, w_down):
    latent_out = lax.map(lambda token: attend_row(token, queries, drafts, cache, lengths, row_seq, row_pos), jnp.arange(TOKENS, dtype=jnp.int32))
    values = jnp.einsum('thl,hlv->thv', latent_out.astype(jnp.float32), w_uv.astype(jnp.float32)).astype(jnp.bfloat16)
    attended = jnp.dot(values.reshape(TOKENS, H * HD), w_out, preferred_element_type=jnp.float32)
    resid = (hidden.astype(jnp.float32) + attended).astype(jnp.bfloat16)
    resid_f = resid.astype(jnp.float32)
    inv_rms = lax.rsqrt(lax.optimization_barrier(jnp.mean(resid_f * resid_f, axis=1, keepdims=True)) + 1e-06)
    scaled = (resid_f * gain[None, :]).astype(jnp.bfloat16)
    gate = jnp.dot(scaled, w_gate, preferred_element_type=jnp.float32) * inv_rms
    up_val = jnp.dot(scaled, w_up, preferred_element_type=jnp.float32) * inv_rms
    act = (jax.nn.silu(gate) * up_val).astype(jnp.bfloat16)
    mixed = resid_f + jnp.dot(act, w_down, preferred_element_type=jnp.float32)
    return mixed.astype(jnp.bfloat16)
```

```python
import functools

import jax
import jax.numpy as jnp
from jax import lax
from jax.experimental import pallas as pl
from jax.experimental.pallas import tpu as pltpu
from jax.sharding import PartitionSpec as P

D, LAT, ROPE, HD = 7168, 512, 64, 128
SEQ_DP, STEPS = 2, 4
W = LAT + ROPE
FF_DEV = 576
DC = 896
BF, F32 = jnp.bfloat16, jnp.float32
C2 = (HD + ROPE) ** (-0.5) * 1.4426950408889634
NEG = -1e30
FLOOR = -20000.0
N_KV, N_DP = 32, 8
N_TILE = 28
KC = 1024
CTX = 4096
NCH = CTX // KC
RB = 32
ROWS = 512
MW = 640
NT = (((1,), (1,)), ((), ()))


def kernel(
    len_ref, seq_ref, pos_ref, qt_hbm, dr_hbm, ct_hbm, wuv_hbm, wout_hbm, hid_hbm, gain_ref, wg_hbm, wu_hbm, wd_hbm,
    out_ref,
    qv, qs0, qs1, kv0, kv1, sc0, sc1, pb0, pb1, mrun, m2, lrun, acc0, acc1,
    drv, wuv, wout, hid, wg, wu, wd,
    send_a, recv_a, send_b, recv_b, send_c, recv_c, send_d, recv_d, send_e, recv_e, send_f, recv_f,
    send_g, recv_g, send_h, recv_h, resid_s,
    ksem, lsem, ssem, rsem,
):
    me = lax.axis_index("kv")
    my_dp = lax.axis_index("dp")
    qss, kvs, scs, pbs, accs = (qs0, qs1), (kv0, kv1), (sc0, sc1), (pb0, pb1), (acc0, acc1)

    def kcopy(s, j):
        return pltpu.make_async_copy(
            ct_hbm.at[s, :, pl.ds(j * KC, KC)], kvs[s].at[:, pl.ds(j * KC, KC)], ksem.at[s, j]
        )

    loads = [
        pltpu.make_async_copy(src, dst, lsem.at[i])
        for i, (src, dst) in enumerate(
            [(qt_hbm, qv), (dr_hbm, drv), (wuv_hbm, wuv), (wout_hbm, wout), (hid_hbm, hid), (wg_hbm, wg), (wu_hbm, wu), (wd_hbm, wd)]
        )
    ]
    loads[0].start()
    for s in range(2):
        for j in range(NCH):
            kcopy(s, j).start()
    for c in loads[1:]:
        c.start()

    barrier = pltpu.get_barrier_semaphore()

    def hello_kv(i, c):
        pl.semaphore_signal(barrier, inc=1, device_id=(lax.rem(me + i, N_KV), my_dp), device_id_type=pl.DeviceIdType.MESH)
        return c

    def hello_dp(i, c):
        pl.semaphore_signal(barrier, inc=1, device_id=(me, lax.rem(my_dp + i, N_DP)), device_id_type=pl.DeviceIdType.MESH)
        return c

    lax.fori_loop(1, N_KV, hello_kv, 0)
    lax.fori_loop(1, N_DP, hello_dp, 0)

    seqs = [seq_ref[t] for t in range(8)]
    ranks = []
    for t in range(8):
        rank = jnp.int32(0)
        for u in range(t):
            rank = rank + (seqs[u] == seqs[t]).astype(jnp.int32)
        ranks.append(rank)
    place = [seqs[t] * STEPS + ranks[t] for t in range(8)]
    idx = []
    for g in range(8):
        at = jnp.int32(0)
        for t in range(8):
            at = at + t * (place[t] == g).astype(jnp.int32)
        idx.append(at)

    pi = lax.broadcasted_iota(jnp.int32, (ROWS, ROWS), 0)
    pj = lax.broadcasted_iota(jnp.int32, (ROWS, ROWS), 1)
    blk = pi >> 4
    want = ((pi >> 2) & 3) * 128 + (((blk & 15) * 2 + (blk >> 4)) * 4) + (pi & 3)
    perm = jnp.where(pj == want, 1.0, 0.0).astype(BF)
    loads[0].wait()

    def sort_q(s):
        qt = jnp.concatenate([qv[idx[s * STEPS + r]] for r in range(STEPS)], axis=1)
        qss[s][...] = lax.dot_general(perm, qt, NT, preferred_element_type=F32).astype(BF)

    starts = [len_ref[s] - me * CTX for s in range(2)]

    def qk(s, j):
        kcopy(s, j).wait()
        r = jnp.dot(qss[s][...], kvs[s][:, j * KC:(j + 1) * KC], preferred_element_type=F32)
        pos = lax.broadcasted_iota(jnp.int32, (1, KC), 1) + j * KC
        r = jnp.where(pos < starts[s], r, NEG)
        scs[s][:, j * KC:(j + 1) * KC] = r
        mx = r[:, :128]
        for c in range(1, KC // 128):
            mx = jnp.maximum(mx, r[:, c * 128:(c + 1) * 128])
        mrun[s] = mx if j == 0 else jnp.maximum(mrun[s], mx)

    def fin(s):
        m = jnp.max(mrun[s], axis=1, keepdims=True) * C2
        m = jnp.maximum(m, FLOOR).astype(BF).astype(F32)
        m2[s] = jnp.broadcast_to(m, (ROWS, 128))

    def pv(s, j, lo, hi):
        for rb in range(lo // RB, hi // RB):
            rows = slice(rb * RB, (rb + 1) * RB)
            mm = m2[s, rows, :]
            l = jnp.zeros((RB, 128), F32) if j == 0 else lrun[s, rows, :]
            for c in range(KC // 128):
                p = jnp.exp2(scs[s][rows, j * KC + c * 128:j * KC + (c + 1) * 128] * C2 - mm)
                l = l + p
                pbs[j % 2][rows, c * 128:(c + 1) * 128] = p.astype(BF)
            lrun[s, rows, :] = l
        r = lax.dot_general(
            pbs[j % 2][lo:hi, :], kvs[s][:LAT, j * KC:(j + 1) * KC], NT, preferred_element_type=F32
        )
        if j == 0:
            accs[s][lo:hi, :] = r
        else:
            accs[s][lo:hi, :] += r

    def ship(s, c):
        rows = slice(c * 256, (c + 1) * 256)
        l = jnp.sum(lrun[s, rows, :], axis=1, keepdims=True)
        l_hi = l.astype(BF).astype(F32)
        lane = lax.broadcasted_iota(jnp.int32, (256, 128), 1)
        ext = jnp.where(lane < 32, m2[s, rows, :], jnp.where(lane < 64, l_hi, l - l_hi))
        send_a[s, c * 16:(c + 1) * 16, :, 0:LAT] = accs[s][rows, :].astype(BF).reshape(16, 16, LAT)
        send_a[s, c * 16:(c + 1) * 16, :, LAT:MW] = ext.astype(BF).reshape(16, 16, 128)

        def one(i, carry):
            chip = lax.rem(lax.div(me, 2) + i, 16)
            to = chip * 2 + c

            @pl.when(to != me)
            def _():
                pltpu.make_async_remote_copy(
                    send_a.at[s, c * 16 + chip], recv_a.at[s, me], ssem.at[0], rsem.at[s],
                    device_id=(to, my_dp), device_id_type=pl.DeviceIdType.MESH,
                ).start()

            @pl.when(to == me)
            def _():
                recv_a[s, me] = send_a[s, c * 16 + chip]

            return carry

        lax.fori_loop(0, 16, one, 0)

    sort_q(0)
    for j in range(NCH):
        qk(0, j)
    fin(0)
    sort_q(1)
    for j in range(NCH):
        qk(1, j)
        pv(0, j, 0, ROWS)
    pl.semaphore_wait(barrier, N_KV - 1 + N_DP - 1)
    ship(0, 0)
    ship(0, 1)
    fin(1)
    for c in range(2):
        for j in range(NCH):
            pv(1, j, c * 256, (c + 1) * 256)
        ship(1, c)

    loads[1].wait()
    drafts = drv[...].astype(F32)
    poss = [pos_ref[t] for t in range(8)]
    posg = [pos_ref[idx[g]] for g in range(8)]
    my_blk = lax.rem(me, 2) * 16 + lax.div(me, 2)
    d_score, d_max = [], []
    rowi = lax.broadcasted_iota(jnp.int32, (16, 1), 0) >> 2
    for s in range(2):
        q_own = qss[s][pl.ds(pl.multiple_of(my_blk * 16, 16), 16), :].astype(F32)
        my_pos = jnp.zeros((16, 1), jnp.int32)
        for r in range(STEPS):
            my_pos = jnp.where(rowi == r, posg[s * STEPS + r], my_pos)
        cols = []
        for t in range(8):
            sct = jnp.sum(q_own * drafts[t:t + 1, :], axis=1, keepdims=True) * C2
            limit = jnp.where(seqs[t] == s, poss[t], jnp.int32(2 ** 30))
            cols.append(jnp.where(my_pos >= limit, sct, NEG))
        d_score.append(cols)
        d_max.append(functools.reduce(jnp.maximum, cols))

    def landed(buf, sem, n):
        view = buf.at[pl.ds(0, n)]
        pltpu.make_async_copy(view, view, sem).wait()

    lats = []
    for s in range(2):
        landed(recv_a.at[s], rsem.at[s], N_KV - 1)
        ext = recv_a[s, :, :, LAT:MW].astype(F32)
        m_k = ext[:, :, 0:1]
        l_k = ext[:, :, 32:33] + ext[:, :, 64:65]
        top = jnp.maximum(jnp.max(m_k, axis=0), d_max[s])
        w_k = jnp.exp2(m_k - top[None])
        den = jnp.sum(w_k * l_k, axis=0)
        num = jnp.zeros((16, LAT), F32)
        for k in range(N_KV):
            num = num + w_k[k] * recv_a[s, k, :, 0:LAT].astype(F32)
        for t in range(8):
            p = jnp.exp2(d_score[s][t] - top)
            den = den + p
            num = num + p.astype(BF).astype(F32) * drafts[t:t + 1, :LAT]
        lats.append((num / den).astype(BF))
    lat = jnp.concatenate(lats, axis=0)

    loads[2].wait()
    hrow = lax.broadcasted_iota(jnp.int32, (32, 1), 0) & 3
    vals = jnp.concatenate(
        [jnp.where(hrow == h, jnp.dot(lat, wuv[h], preferred_element_type=F32), 0.0) for h in range(4)], axis=1
    ).astype(BF)
    ut = lax.broadcasted_iota(jnp.int32, (8, 32), 0)
    uc = lax.broadcasted_iota(jnp.int32, (8, 32), 1) >> 2
    want_at = jnp.zeros((8, 32), jnp.int32)
    for t in range(8):
        want_at = jnp.where(ut == t, place[t], want_at)
    unsort = jnp.where(uc == want_at, 1.0, 0.0).astype(BF)
    v8 = jnp.dot(unsort, vals, preferred_element_type=F32)
    send_b[...] = jnp.concatenate([v8[:, :256], v8[:, 256:]], axis=0).astype(BF)
    recv_b[my_dp] = send_b[...]

    def over_dp(src, dst, s_sem, r_sem):
        def one(i, c):
            to = lax.rem(my_dp + i, N_DP)
            pltpu.make_async_remote_copy(
                src(to), dst.at[my_dp], s_sem, r_sem, device_id=(me, to), device_id_type=pl.DeviceIdType.MESH
            ).start()
            return c

        lax.fori_loop(1, N_DP, one, 0)

    def scatter_kv(src, dst, s_sem, r_sem):
        def one(i, c):
            to = lax.rem(me + i, N_KV)

            @pl.when(to < N_TILE)
            def _():
                pltpu.make_async_remote_copy(
                    src.at[to], dst.at[me], s_sem, r_sem, device_id=(to, my_dp), device_id_type=pl.DeviceIdType.MESH
                ).start()

            return c

        lax.fori_loop(1, N_KV, one, 0)

    def gather_kv(src, dst, s_sem, r_sem):
        def one(i, c):
            to = lax.rem(me + i, N_KV)
            pltpu.make_async_remote_copy(
                src, dst.at[me], s_sem, r_sem, device_id=(to, my_dp), device_id_type=pl.DeviceIdType.MESH
            ).start()
            return c

        lax.fori_loop(1, N_KV, one, 0)

    def tiles(x, buf):
        xb = x.astype(BF)
        for rc in range(4):
            for ct in range(7):
                buf[rc * 7 + ct] = xb[rc * 16:(rc + 1) * 16, ct * 128:(ct + 1) * 128]

    def whole(buf):
        return jnp.concatenate(
            [jnp.concatenate([buf[rc * 7 + ct].astype(F32) for ct in range(7)], axis=1) for rc in range(4)], axis=0
        )

    over_dp(lambda to: send_b, recv_b, ssem.at[1], rsem.at[2])
    landed(recv_b, rsem.at[2], N_DP - 1)
    loads[3].wait()
    all_vals = []
    for d in range(N_DP):
        both = recv_b[d].astype(F32)
        all_vals.append(jnp.concatenate([both[:8], both[8:]], axis=1))
    all_vals = jnp.concatenate(all_vals, axis=0).astype(BF)
    tiles(jnp.dot(all_vals, wout[...], preferred_element_type=F32), send_c)
    scatter_kv(send_c, recv_c, ssem.at[2], rsem.at[3])
    loads[4].wait()

    @pl.when(me < N_TILE)
    def _():
        recv_c[me] = send_c[me]
        landed(recv_c, rsem.at[3], N_KV - 1)
        total = jnp.sum(recv_c[...].astype(F32), axis=0)
        rc, ct = lax.div(me, 7), lax.rem(me, 7)
        own = hid[pl.ds(pl.multiple_of(rc * 16, 16), 16), pl.ds(pl.multiple_of(ct * 128, 128), 128)]
        send_d[...] = (own.astype(F32) + total).astype(BF)
        recv_d[me] = send_d[...]
        gather_kv(send_d, recv_d, ssem.at[3], rsem.at[4])
        landed(recv_d, rsem.at[4], N_TILE - 1)

    @pl.when(me >= N_TILE)
    def _():
        landed(recv_d, rsem.at[4], N_TILE)

    resid = whole(recv_d)
    square = jnp.sum(resid * resid, axis=1, keepdims=True)
    sq_hi = square.astype(BF).astype(F32)
    scaled = (resid * gain_ref[...]).astype(BF)
    loads[5].wait()
    loads[6].wait()
    gate = lax.dot_general(scaled, wg[...], NT, preferred_element_type=F32)
    up = lax.dot_general(scaled, wu[...], NT, preferred_element_type=F32)
    gate = jnp.concatenate([gate, jnp.broadcast_to(sq_hi, (64, MW - FF_DEV))], axis=1)
    up = jnp.concatenate([up, jnp.broadcast_to(square - sq_hi, (64, MW - FF_DEV))], axis=1)
    for d in range(N_DP):
        rows = slice(d * 8, (d + 1) * 8)
        send_e[d] = jnp.concatenate([gate[rows], up[rows]], axis=0).astype(BF)
    over_dp(lambda to: send_e.at[to], recv_e, ssem.at[4], rsem.at[5])
    recv_e[my_dp] = send_e[my_dp]
    landed(recv_e, rsem.at[5], N_DP - 1)
    total = jnp.sum(recv_e[...].astype(F32), axis=0)
    sq = total[0:8, FF_DEV:FF_DEV + 1] + total[8:16, FF_DEV:FF_DEV + 1]
    inv = lax.rsqrt(sq / D + 1e-06)
    g = total[0:8, :FF_DEV] * inv
    u = total[8:16, :FF_DEV] * inv
    act = g / (1.0 + jnp.exp(-g)) * u
    right = jnp.concatenate([act[:, 384:], jnp.zeros((8, 192), F32)], axis=1)
    send_f[...] = jnp.concatenate([act[:, :384], right], axis=0).astype(BF)
    recv_f[my_dp] = send_f[...]
    over_dp(lambda to: send_f, recv_f, ssem.at[5], rsem.at[6])
    landed(recv_f, rsem.at[6], N_DP - 1)
    acts = []
    for d in range(N_DP):
        both = recv_f[d].astype(F32)
        acts.append(jnp.concatenate([both[:8], both[8:, :192]], axis=1))
    acts = jnp.concatenate(acts, axis=0).astype(BF)
    loads[7].wait()
    tiles(jnp.dot(acts, wd[...], preferred_element_type=F32), send_g)
    scatter_kv(send_g, recv_g, ssem.at[6], rsem.at[7])

    @pl.when(me < N_TILE)
    def _():
        recv_g[me] = send_g[me]
        landed(recv_g, rsem.at[7], N_KV - 1)
        total = jnp.sum(recv_g[...].astype(F32), axis=0)
        send_h[...] = (send_d[...].astype(F32) + total).astype(BF)
        recv_h[me] = send_h[...]
        gather_kv(send_h, recv_h, ssem.at[7], rsem.at[8])
        landed(recv_h, rsem.at[8], N_TILE - 1)

    @pl.when(me >= N_TILE)
    def _():
        landed(recv_h, rsem.at[8], N_TILE)

    for rc in range(4):
        for ct in range(7):
            out_ref[rc * 16:(rc + 1) * 16, ct * 128:(ct + 1) * 128] = recv_h[rc * 7 + ct]

    for s in range(2):
        landed(send_a.at[s], ssem.at[0], N_KV - 1)
    landed(recv_b, ssem.at[1], N_DP - 1)
    landed(recv_e, ssem.at[4], N_DP - 1)
    landed(recv_f, ssem.at[5], N_DP - 1)

    @pl.when(me < N_TILE)
    def _():
        landed(send_c, ssem.at[2], N_TILE - 1)
        landed(send_g, ssem.at[6], N_TILE - 1)
        landed(recv_c, ssem.at[3], N_KV - 1)
        landed(recv_g, ssem.at[7], N_KV - 1)

    @pl.when(me >= N_TILE)
    def _():
        landed(send_c, ssem.at[2], N_TILE)
        landed(send_g, ssem.at[6], N_TILE)


def on_device(queries, drafts, cache, lengths, row_seq, row_pos, w_uv, w_out, hidden, gain, w_gate, w_up, w_down):
    smem = pl.BlockSpec(memory_space=pltpu.SMEM)
    vmem = pl.BlockSpec(memory_space=pltpu.VMEM)
    hbm = pl.BlockSpec(memory_space=pl.ANY)
    v = pltpu.VMEM
    scratch = [
        v((8, W, 128), BF), v((ROWS, W), BF), v((ROWS, W), BF), v((W, CTX), BF), v((W, CTX), BF),
        v((ROWS, CTX), F32), v((ROWS, CTX), F32), v((ROWS, KC), BF), v((ROWS, KC), BF),
        v((2, ROWS, 128), F32), v((2, ROWS, 128), F32), v((2, ROWS, 128), F32), v((ROWS, LAT), F32), v((ROWS, LAT), F32),
        v((8, W), BF), v((4, LAT, HD), BF), v((4 * HD, DC), BF), v((64, DC), BF), v((FF_DEV, DC), BF), v((FF_DEV, DC), BF), v((FF_DEV, DC), BF),
        v((2, 32, 16, MW), BF), v((2, 32, 16, MW), BF),
        v((16, 256), BF), v((N_DP, 16, 256), BF),
        v((N_TILE, 16, 128), BF), v((N_KV, 16, 128), BF),
        v((16, 128), BF), v((N_TILE, 16, 128), BF),
        v((N_DP, 16, MW), BF), v((N_DP, 16, MW), BF),
        v((16, 384), BF), v((N_DP, 16, 384), BF),
        v((N_TILE, 16, 128), BF), v((N_KV, 16, 128), BF),
        v((16, 128), BF), v((N_TILE, 16, 128), BF), v((8, 128), F32),
        pltpu.SemaphoreType.DMA((2, NCH)), pltpu.SemaphoreType.DMA((8,)), pltpu.SemaphoreType.DMA((8,)), pltpu.SemaphoreType.DMA((9,)),
    ]
    return pl.pallas_call(
        kernel,
        out_shape=jax.ShapeDtypeStruct((64, DC), BF),
        in_specs=[smem] * 3 + [hbm] * 6 + [vmem] + [hbm] * 3,
        out_specs=vmem,
        scratch_shapes=scratch,
        compiler_params=pltpu.CompilerParams(
            collective_id=0, has_side_effects=True, vmem_limit_bytes=58 << 20
        ),
        name="verify_layer",
    )(
        lengths, row_seq, row_pos, jnp.swapaxes(queries, 1, 2), drafts, jnp.swapaxes(cache, 1, 2), w_uv, w_out, hidden,
        gain.reshape(1, DC), w_gate.T, w_up.T, w_down,
    )


def solution(mesh):
    placed = (
        P("dp", None, None),
        P("dp", None),
        P("dp", "kv", None),
        P("dp"),
        P("dp"),
        P("dp"),
        P("kv", None, None),
        P("kv", "dp"),
        P(None, "dp"),
        P("dp"),
        P("dp", "kv"),
        P("dp", "kv"),
        P("kv", "dp"),
    )
    return jax.shard_map(
        on_device, mesh=mesh, in_specs=placed, out_specs=P(None, "dp"), check_vma=False
    )
```

```python
import functools

import jax
import jax.numpy as jnp
from jax import lax
from jax.experimental import pallas as pl
from jax.experimental.pallas import tpu as pltpu
from jax.sharding import PartitionSpec as P

D, LAT, ROPE, HD = 7168, 512, 64, 128
SEQ_DP, STEPS = 2, 4
W = LAT + ROPE
FF_DEV = 576
DC = 896
BF, F32 = jnp.bfloat16, jnp.float32
C2 = (HD + ROPE) ** (-0.5) * 1.4426950408889634
NEG = -1e30
FLOOR = -20000.0
N_KV, N_DP = 32, 8
N_TILE = 28
KC = 1024
CTX = 4096
NCH = CTX // KC
RB = 32
ROWS = 512
MW = 640
NT = (((1,), (1,)), ((), ()))
Z_FAR = (4, 3, 5, 2, 6, 1, 7)
XY_FAR = sorted(((dx, dy) for dx in range(4) for dy in range(4)), key=lambda o: -(min(o[0], 4 - o[0]) + min(o[1], 4 - o[1])))
KV_FAR = [(dx, dy, dc) for dx, dy in XY_FAR for dc in (0, 1)][:-2] + [(0, 0, 1)]


def kernel(
    len_ref, seq_ref, pos_ref, qt_hbm, dr_hbm, ct_hbm, wuv_hbm, wout_hbm, hid_hbm, gain_ref, wg_hbm, wu_hbm, wd_hbm,
    out_ref,
    qv, qs0, qs1, kv0, kv1, sc0, sc1, pb0, pb1, mrun, m2, lrun, acc0, acc1,
    drv, wuv, wout, hid, wg, wu, wd,
    send_s, recv_s, send_a, recv_a, send_b, recv_b, send_c, recv_c, send_d, recv_d, send_e, recv_e, send_f, recv_f,
    send_g, recv_g, send_h,
    ksem, lsem, ssem, rsem,
):
    me = lax.axis_index("kv")
    my_dp = lax.axis_index("dp")
    my_core = lax.rem(me, 2)
    my_chip = lax.div(me, 2)
    xs = [lax.rem(lax.div(me, 8) + dx, 4) * 8 for dx in range(4)]
    ys = [lax.rem(lax.rem(my_chip, 4) + dy, 4) * 2 for dy in range(4)]
    cs = [lax.rem(me + dc, 2) for dc in range(2)]
    qss, kvs, scs, pbs, accs = (qs0, qs1), (kv0, kv1), (sc0, sc1), (pb0, pb1), (acc0, acc1)

    def kcopy(s, j):
        return pltpu.make_async_copy(
            ct_hbm.at[s, :, pl.ds(j * KC, KC)], kvs[s].at[:, pl.ds(j * KC, KC)], ksem.at[s, j]
        )

    loads = [
        pltpu.make_async_copy(src, dst, lsem.at[i])
        for i, (src, dst) in enumerate(
            [(qt_hbm, qv), (dr_hbm, drv), (wuv_hbm, wuv), (wout_hbm, wout), (hid_hbm, hid), (wg_hbm, wg), (wu_hbm, wu), (wd_hbm, wd)]
        )
    ]
    loads[0].start()
    for s in range(2):
        for j in range(NCH):
            kcopy(s, j).start()
    for c in loads[1:]:
        c.start()

    barrier = pltpu.get_barrier_semaphore()

    def hello():
        for dx, dy, dc in KV_FAR:
            pl.semaphore_signal(
                barrier, inc=1, device_id=(xs[dx] + ys[dy] + cs[dc], my_dp), device_id_type=pl.DeviceIdType.MESH
            )
        for dz in Z_FAR:
            pl.semaphore_signal(
                barrier, inc=1, device_id=(me, lax.rem(my_dp + dz, N_DP)), device_id_type=pl.DeviceIdType.MESH
            )

    hello()

    seqs = [seq_ref[t] for t in range(8)]
    ranks = []
    for t in range(8):
        rank = jnp.int32(0)
        for u in range(t):
            rank = rank + (seqs[u] == seqs[t]).astype(jnp.int32)
        ranks.append(rank)
    place = [seqs[t] * STEPS + ranks[t] for t in range(8)]
    idx = []
    for g in range(8):
        at = jnp.int32(0)
        for t in range(8):
            at = at + t * (place[t] == g).astype(jnp.int32)
        idx.append(at)

    pi = lax.broadcasted_iota(jnp.int32, (ROWS, 128), 0)
    pj = lax.broadcasted_iota(jnp.int32, (ROWS, 128), 1)
    blk = (pi >> 4) & 15
    owner = jnp.where(pi < 256, cs[1], cs[0])
    for b, (dx, dy) in enumerate(XY_FAR):
        owner = owner + jnp.where(blk == b, xs[dx] + ys[dy], 0)
    want = ((pi >> 2) & 3) * 128 + owner * 4 + (pi & 3)
    perm = jnp.concatenate([jnp.where(pj + 128 * r == want, 1.0, 0.0).astype(BF) for r in range(STEPS)], axis=1)
    loads[0].wait()

    def sort_q(s):
        qt = jnp.concatenate([qv[idx[s * STEPS + r]] for r in range(STEPS)], axis=1)
        qss[s][...] = lax.dot_general(perm, qt, NT, preferred_element_type=F32).astype(BF)

    starts = [len_ref[s] - me * CTX for s in range(2)]

    def qk(s, j):
        kcopy(s, j).wait()
        r = jnp.dot(qss[s][...], kvs[s][:, j * KC:(j + 1) * KC], preferred_element_type=F32)
        pos = lax.broadcasted_iota(jnp.int32, (1, KC), 1) + j * KC
        r = jnp.where(pos < starts[s], r, NEG)
        scs[s][:, j * KC:(j + 1) * KC] = r
        mx = r[:, :128]
        for c in range(1, KC // 128):
            mx = jnp.maximum(mx, r[:, c * 128:(c + 1) * 128])
        mrun[s] = mx if j == 0 else jnp.maximum(mrun[s], mx)

    def fin(s):
        m = jnp.max(mrun[s], axis=1, keepdims=True) * C2
        m = jnp.maximum(m, FLOOR).astype(BF).astype(F32)
        m2[s] = jnp.broadcast_to(m, (ROWS, 128))

    def pv(s, j, lo, hi):
        for rb in range(lo // RB, hi // RB):
            rows = slice(rb * RB, (rb + 1) * RB)
            mm = m2[s, rows, :]
            l = jnp.zeros((RB, 128), F32) if j == 0 else lrun[s, rows, :]
            for c in range(KC // 128):
                p = jnp.exp2(scs[s][rows, j * KC + c * 128:j * KC + (c + 1) * 128] * C2 - mm)
                l = l + p
                pbs[j % 2][rows, c * 128:(c + 1) * 128] = p.astype(BF)
            lrun[s, rows, :] = l
        r = lax.dot_general(
            pbs[j % 2][lo:hi, :], kvs[s][:LAT, j * KC:(j + 1) * KC], NT, preferred_element_type=F32
        )
        if j == 0:
            accs[s][lo:hi, :] = r
        else:
            accs[s][lo:hi, :] += r

    def landed(buf, sem, n):
        view = buf.at[pl.ds(0, n)]
        pltpu.make_async_copy(view, view, sem).wait()

    def pack(buf, acc, m, l):
        lane = lax.broadcasted_iota(jnp.int32, m.shape, 1)
        l_hi = l.astype(BF).astype(F32)
        ext = jnp.where(lane < 32, m, jnp.where(lane < 64, l_hi, l - l_hi))
        buf[:, :, 0:LAT] = acc.astype(BF).reshape(-1, 16, LAT)
        buf[:, :, LAT:MW] = ext.astype(BF).reshape(-1, 16, 128)

    def total(s, rows):
        return jnp.sum(lrun[s, rows, :], axis=1, keepdims=True)

    def to_sibling(s):
        rows = slice(0, 256)
        pack(send_s.at[s], accs[s][rows, :], m2[s, rows, :], total(s, rows))
        pltpu.make_async_remote_copy(
            send_s.at[s], recv_s.at[s], ssem.at[8], rsem.at[9 + s], device_id=(xs[0] + ys[0] + cs[1], my_dp),
            device_id_type=pl.DeviceIdType.MESH,
        ).start()

    def to_owners(s, lo, hi):
        rows = slice(256 + lo * 16, 256 + hi * 16)
        m_a = m2[s, rows, :]
        ext = recv_s[s, lo:hi, :, LAT:MW].astype(F32).reshape(-1, 128)
        m_b = ext[:, 0:1]
        l_b = ext[:, 32:33] + ext[:, 64:65]
        top = jnp.maximum(m_a, m_b)
        w_a = jnp.exp2(m_a - top)
        w_b = jnp.exp2(m_b - top)
        acc = accs[s][rows, :] * w_a[:, 0:1] + recv_s[s, lo:hi, :, 0:LAT].astype(F32).reshape(-1, LAT) * w_b[:, 0:1]
        pack(send_a.at[s, lo:hi], acc, top, total(s, rows) * w_a + l_b * w_b)
        for b in range(lo, min(hi, 15)):
            dx, dy = XY_FAR[b]
            pltpu.make_async_remote_copy(
                send_a.at[s, b], recv_a.at[s, b], ssem.at[0], rsem.at[s], device_id=(xs[dx] + ys[dy] + cs[0], my_dp),
                device_id_type=pl.DeviceIdType.MESH,
            ).start()
        if hi == 16:
            recv_a[s, 15] = send_a[s, 15]

    sort_q(0)
    for j in range(NCH):
        qk(0, j)
    fin(0)
    sort_q(1)
    for j in range(NCH):
        if j % 2 == 0:
            qk(1, j // 2)
        pv(0, j, 0, ROWS)
    pl.semaphore_wait(barrier, N_KV - 1 + N_DP - 1)
    to_sibling(0)
    qk(1, 2)
    qk(1, 3)
    landed(recv_s.at[0], rsem.at[9], 16)
    to_owners(0, 0, 16)
    fin(1)
    for j in range(NCH):
        pv(1, j, 0, 256)
    to_sibling(1)
    for j in range(NCH):
        pv(1, j, 256, 384)
    landed(recv_s.at[1], rsem.at[10], 16)
    to_owners(1, 0, 8)
    for j in range(NCH):
        pv(1, j, 384, 512)
    to_owners(1, 8, 16)

    loads[1].wait()
    drafts = drv[...].astype(F32)
    poss = [pos_ref[t] for t in range(8)]
    posg = [pos_ref[idx[g]] for g in range(8)]
    d_score, d_max = [], []
    rowi = lax.broadcasted_iota(jnp.int32, (16, 1), 0) >> 2
    for s in range(2):
        q_own = qss[s][496:512, :].astype(F32)
        my_pos = jnp.zeros((16, 1), jnp.int32)
        for r in range(STEPS):
            my_pos = jnp.where(rowi == r, posg[s * STEPS + r], my_pos)
        cols = []
        for t in range(8):
            sct = jnp.sum(q_own * drafts[t:t + 1, :], axis=1, keepdims=True) * C2
            limit = jnp.where(seqs[t] == s, poss[t], jnp.int32(2 ** 30))
            cols.append(jnp.where(my_pos >= limit, sct, NEG))
        d_score.append(cols)
        d_max.append(functools.reduce(jnp.maximum, cols))

    lats = []
    for s in range(2):
        landed(recv_a.at[s], rsem.at[s], 15)
        ext = recv_a[s, :, :, LAT:MW].astype(F32)
        m_k = ext[:, :, 0:1]
        l_k = ext[:, :, 32:33] + ext[:, :, 64:65]
        top = jnp.maximum(jnp.max(m_k, axis=0), d_max[s])
        w_k = jnp.exp2(m_k - top[None])
        den = jnp.sum(w_k * l_k, axis=0)
        num = jnp.zeros((16, LAT), F32)
        for k in range(16):
            num = num + w_k[k] * recv_a[s, k, :, 0:LAT].astype(F32)
        for t in range(8):
            p = jnp.exp2(d_score[s][t] - top)
            den = den + p
            num = num + p.astype(BF).astype(F32) * drafts[t:t + 1, :LAT]
        lats.append((num / den).astype(BF))
    lat = jnp.concatenate(lats, axis=0)

    loads[2].wait()
    hrow = lax.broadcasted_iota(jnp.int32, (32, 1), 0) & 3
    vals = jnp.concatenate(
        [jnp.where(hrow == h, jnp.dot(lat, wuv[h], preferred_element_type=F32), 0.0) for h in range(4)], axis=1
    ).astype(BF)
    ut = lax.broadcasted_iota(jnp.int32, (8, 32), 0)
    uc = lax.broadcasted_iota(jnp.int32, (8, 32), 1) >> 2
    want_at = jnp.zeros((8, 32), jnp.int32)
    for t in range(8):
        want_at = jnp.where(ut == t, place[t], want_at)
    unsort = jnp.where(uc == want_at, 1.0, 0.0).astype(BF)
    v8 = jnp.dot(unsort, vals, preferred_element_type=F32)
    send_b[...] = jnp.concatenate([v8[:, :256], v8[:, 256:]], axis=0).astype(BF)
    recv_b[my_dp] = send_b[...]

    def over_dp(src, dst, s_sem, r_sem):
        for dz in Z_FAR:
            to = lax.rem(my_dp + dz, N_DP)
            pltpu.make_async_remote_copy(
                src(to), dst.at[my_dp], s_sem, r_sem, device_id=(me, to), device_id_type=pl.DeviceIdType.MESH
            ).start()

    def scatter_kv(src, dst, s_sem, r_sem):
        for dx, dy, dc in KV_FAR:
            to = xs[dx] + ys[dy] + cs[dc]

            @pl.when(to < N_TILE)
            def _():
                pltpu.make_async_remote_copy(
                    src.at[to], dst.at[me], s_sem, r_sem, device_id=(to, my_dp), device_id_type=pl.DeviceIdType.MESH
                ).start()

    def gather_kv(src, dst, s_sem, r_sem):
        for dx, dy, dc in KV_FAR:
            to = xs[dx] + ys[dy] + cs[dc]
            pltpu.make_async_remote_copy(
                src, dst.at[me], s_sem, r_sem, device_id=(to, my_dp), device_id_type=pl.DeviceIdType.MESH
            ).start()

    def tiles(x, buf):
        xb = x.astype(BF)
        for rc in range(4):
            for ct in range(7):
                buf[rc * 7 + ct] = xb[rc * 16:(rc + 1) * 16, ct * 128:(ct + 1) * 128]

    def whole(buf):
        return jnp.concatenate(
            [jnp.concatenate([buf[rc * 7 + ct].astype(F32) for ct in range(7)], axis=1) for rc in range(4)], axis=0
        )

    over_dp(lambda to: send_b, recv_b, ssem.at[1], rsem.at[2])
    landed(recv_b, rsem.at[2], N_DP - 1)
    loads[3].wait()
    all_vals = []
    for d in range(N_DP):
        both = recv_b[d].astype(F32)
        all_vals.append(jnp.concatenate([both[:8], both[8:]], axis=1))
    all_vals = jnp.concatenate(all_vals, axis=0).astype(BF)
    tiles(jnp.dot(all_vals, wout[...], preferred_element_type=F32), send_c)
    scatter_kv(send_c, recv_c, ssem.at[2], rsem.at[3])
    loads[4].wait()

    @pl.when(me < N_TILE)
    def _():
        recv_c[me] = send_c[me]
        landed(recv_c, rsem.at[3], N_KV - 1)
        total = jnp.sum(recv_c[...].astype(F32), axis=0)
        rc, ct = lax.div(me, 7), lax.rem(me, 7)
        own = hid[pl.ds(pl.multiple_of(rc * 16, 16), 16), pl.ds(pl.multiple_of(ct * 128, 128), 128)]
        send_d[...] = (own.astype(F32) + total).astype(BF)
        recv_d[me] = send_d[...]
        gather_kv(send_d, recv_d, ssem.at[3], rsem.at[4])
        landed(recv_d, rsem.at[4], N_TILE - 1)

    @pl.when(me >= N_TILE)
    def _():
        landed(recv_d, rsem.at[4], N_TILE)

    resid = whole(recv_d)
    square = jnp.sum(resid * resid, axis=1, keepdims=True)
    sq_hi = square.astype(BF).astype(F32)
    scaled = (resid * gain_ref[...][None, :]).astype(BF)
    loads[5].wait()
    loads[6].wait()
    gate = lax.dot_general(scaled, wg[...], NT, preferred_element_type=F32)
    up = lax.dot_general(scaled, wu[...], NT, preferred_element_type=F32)
    gate = jnp.concatenate([gate, jnp.broadcast_to(sq_hi, (64, MW - FF_DEV))], axis=1)
    up = jnp.concatenate([up, jnp.broadcast_to(square - sq_hi, (64, MW - FF_DEV))], axis=1)
    for d in range(N_DP):
        rows = slice(d * 8, (d + 1) * 8)
        send_e[d] = jnp.concatenate([gate[rows], up[rows]], axis=0).astype(BF)
    over_dp(lambda to: send_e.at[to], recv_e, ssem.at[4], rsem.at[5])
    recv_e[my_dp] = send_e[my_dp]
    landed(recv_e, rsem.at[5], N_DP - 1)
    total = jnp.sum(recv_e[...].astype(F32), axis=0)
    sq = total[0:8, FF_DEV:FF_DEV + 1] + total[8:16, FF_DEV:FF_DEV + 1]
    inv = lax.rsqrt(sq / D + 1e-06)
    g = total[0:8, :FF_DEV] * inv
    u = total[8:16, :FF_DEV] * inv
    act = g / (1.0 + jnp.exp(-g)) * u
    right = jnp.concatenate([act[:, 384:], jnp.zeros((8, 192), F32)], axis=1)
    send_f[...] = jnp.concatenate([act[:, :384], right], axis=0).astype(BF)
    recv_f[my_dp] = send_f[...]
    over_dp(lambda to: send_f, recv_f, ssem.at[5], rsem.at[6])
    landed(recv_f, rsem.at[6], N_DP - 1)
    acts = []
    for d in range(N_DP):
        both = recv_f[d].astype(F32)
        acts.append(jnp.concatenate([both[:8], both[8:, :192]], axis=1))
    acts = jnp.concatenate(acts, axis=0).astype(BF)
    loads[7].wait()
    tiles(jnp.dot(acts, wd[...], preferred_element_type=F32), send_g)
    scatter_kv(send_g, recv_g, ssem.at[6], rsem.at[7])

    @pl.when(me < N_TILE)
    def _():
        recv_g[me] = send_g[me]
        landed(recv_g, rsem.at[7], N_KV - 1)
        total = jnp.sum(recv_g[...].astype(F32), axis=0)
        send_h[...] = (send_d[...].astype(F32) + total).astype(BF)
        gather_kv(send_h, out_ref, ssem.at[7], rsem.at[8])
        mine = pltpu.make_async_copy(send_h, out_ref.at[me], lsem.at[8])
        mine.start()
        mine.wait()
        landed(out_ref, rsem.at[8], N_TILE - 1)

    @pl.when(me >= N_TILE)
    def _():
        landed(out_ref, rsem.at[8], N_TILE)


    for s in range(2):
        landed(send_a.at[s], ssem.at[0], 15)
        landed(send_s.at[s], ssem.at[8], 16)
    landed(recv_b, ssem.at[1], N_DP - 1)
    landed(recv_e, ssem.at[4], N_DP - 1)
    landed(recv_f, ssem.at[5], N_DP - 1)

    @pl.when(me < N_TILE)
    def _():
        landed(send_c, ssem.at[2], N_TILE - 1)
        landed(send_g, ssem.at[6], N_TILE - 1)
        landed(recv_c, ssem.at[3], N_KV - 1)
        landed(recv_g, ssem.at[7], N_KV - 1)

    @pl.when(me >= N_TILE)
    def _():
        landed(send_c, ssem.at[2], N_TILE)
        landed(send_g, ssem.at[6], N_TILE)


def on_device(queries, drafts, cache, lengths, row_seq, row_pos, w_uv, w_out, hidden, gain, w_gate, w_up, w_down):
    smem = pl.BlockSpec(memory_space=pltpu.SMEM)
    vmem = pl.BlockSpec(memory_space=pltpu.VMEM)
    hbm = pl.BlockSpec(memory_space=pl.ANY)
    v = pltpu.VMEM
    scratch = [
        v((8, W, 128), BF), v((ROWS, W), BF), v((ROWS, W), BF), v((W, CTX), BF), v((W, CTX), BF),
        v((ROWS, CTX), F32), v((ROWS, CTX), F32), v((ROWS, KC), BF), v((ROWS, KC), BF),
        v((2, ROWS, 128), F32), v((2, ROWS, 128), F32), v((2, ROWS, 128), F32), v((ROWS, LAT), F32), v((ROWS, LAT), F32),
        v((8, W), BF), v((4, LAT, HD), BF), v((4 * HD, DC), BF), v((64, DC), BF), v((FF_DEV, DC), BF), v((FF_DEV, DC), BF), v((FF_DEV, DC), BF),
        v((2, 16, 16, MW), BF), v((2, 16, 16, MW), BF), v((2, 16, 16, MW), BF), v((2, 16, 16, MW), BF),
        v((16, 256), BF), v((N_DP, 16, 256), BF),
        v((N_TILE, 16, 128), BF), v((N_KV, 16, 128), BF),
        v((16, 128), BF), v((N_TILE, 16, 128), BF),
        v((N_DP, 16, MW), BF), v((N_DP, 16, MW), BF),
        v((16, 384), BF), v((N_DP, 16, 384), BF),
        v((N_TILE, 16, 128), BF), v((N_KV, 16, 128), BF),
        v((16, 128), BF),
        pltpu.SemaphoreType.DMA((2, NCH)), pltpu.SemaphoreType.DMA((9,)), pltpu.SemaphoreType.DMA((9,)), pltpu.SemaphoreType.DMA((11,)),
    ]
    out = pl.pallas_call(
        kernel,
        out_shape=jax.ShapeDtypeStruct((N_TILE, 16, 128), BF),
        in_specs=[smem] * 3 + [hbm] * 6 + [vmem] + [hbm] * 3,
        out_specs=hbm,
        scratch_shapes=scratch,
        compiler_params=pltpu.CompilerParams(
            collective_id=0, has_side_effects=True, vmem_limit_bytes=60 << 20
        ),
        name="verify_layer",
    )(
        lengths, row_seq, row_pos, jnp.swapaxes(queries, 1, 2), drafts, jnp.swapaxes(cache, 1, 2), w_uv, w_out, hidden,
        gain, w_gate.T, w_up.T, w_down,
    )
    return out.reshape(4, 7, 16, 128).swapaxes(1, 2).reshape(64, DC)


def solution(mesh):
    placed = (
        P("dp", None, None),
        P("dp", None),
        P("dp", "kv", None),
        P("dp"),
        P("dp"),
        P("dp"),
        P("kv", None, None),
        P("kv", "dp"),
        P(None, "dp"),
        P("dp"),
        P("dp", "kv"),
        P("dp", "kv"),
        P("kv", "dp"),
    )
    return jax.shard_map(
        on_device, mesh=mesh, in_specs=placed, out_specs=P(None, "dp"), check_vma=False
    )
```

```python
import functools

import jax
import jax.numpy as jnp
from jax import lax
from jax.experimental import pallas as pl
from jax.experimental.pallas import tpu as pltpu
from jax.sharding import PartitionSpec as P

D, LAT, ROPE, HD = 7168, 512, 64, 128
SEQ_DP, STEPS = 2, 4
W = LAT + ROPE
FF_DEV = 576
DC = 896
BF, F32 = jnp.bfloat16, jnp.float32
C2 = (HD + ROPE) ** (-0.5) * 1.4426950408889634
NEG = -1e30
FLOOR = -20000.0
N_KV, N_DP = 32, 8
N_TILE = 28
KC = 1024
CTX = 4096
NCH = CTX // KC
KP = 2048
NPV = CTX // KP
RB = 32
ROWS = 512
MW = 640
NT = (((1,), (1,)), ((), ()))
Z_FAR = (4, 3, 5, 2, 6, 1, 7)
XY_FAR = sorted(((dx, dy) for dx in range(4) for dy in range(4)), key=lambda o: -(min(o[0], 4 - o[0]) + min(o[1], 4 - o[1])))
KV_FAR = [(dx, dy, dc) for dx, dy in XY_FAR for dc in (0, 1)][:-2] + [(0, 0, 1)]


def kernel(
    len_ref, seq_ref, pos_ref, qt_hbm, dr_hbm, ct_hbm, wuv_hbm, wout_hbm, hid_hbm, gain_ref, wg_hbm, wu_hbm, wd_hbm,
    out_ref,
    qv, qs0, qs1, kv0, kv1, sc0, sc1, pb0, pb1, mrun, m2, lrun, acc0, acc1,
    drv, wuv, wout, hid, wg, wu, wd, wgt, wut,
    send_s, recv_s, send_a, recv_a, send_b, recv_b, send_c, recv_c, send_d, recv_d, send_e, recv_e, send_x, recv_x, send_f, recv_f,
    send_g, recv_g, send_h, count_h,
    ksem, lsem, ssem, rsem,
):
    me = lax.axis_index("kv")
    my_dp = lax.axis_index("dp")
    my_core = lax.rem(me, 2)
    my_chip = lax.div(me, 2)
    xs = [lax.rem(lax.div(me, 8) + dx, 4) * 8 for dx in range(4)]
    ys = [lax.rem(lax.rem(my_chip, 4) + dy, 4) * 2 for dy in range(4)]
    cs = [lax.rem(me + dc, 2) for dc in range(2)]
    qss, kvs, scs, pbs, accs = (qs0, qs1), (kv0, kv1), (sc0, sc1), (pb0, pb1), (acc0, acc1)

    def kcopy(s, j):
        return pltpu.make_async_copy(
            ct_hbm.at[s, :, pl.ds(j * KC, KC)], kvs[s].at[:, pl.ds(j * KC, KC)], ksem.at[s, j]
        )

    loads = [
        pltpu.make_async_copy(src, dst, lsem.at[i])
        for i, (src, dst) in enumerate(
            [(qt_hbm, qv), (dr_hbm, drv), (wuv_hbm, wuv), (wout_hbm, wout), (hid_hbm, hid), (wg_hbm, wg), (wu_hbm, wu), (wd_hbm, wd)]
        )
    ]
    loads[0].start()
    for s in range(2):
        for j in range(NCH):
            kcopy(s, j).start()
    for c in loads[1:]:
        c.start()

    barrier = pltpu.get_barrier_semaphore()

    def hello():
        for dx, dy, dc in KV_FAR:
            pl.semaphore_signal(
                barrier, inc=1, device_id=(xs[dx] + ys[dy] + cs[dc], my_dp), device_id_type=pl.DeviceIdType.MESH
            )
        for dz in Z_FAR:
            pl.semaphore_signal(
                barrier, inc=1, device_id=(me, lax.rem(my_dp + dz, N_DP)), device_id_type=pl.DeviceIdType.MESH
            )

    hello()

    seqs = [seq_ref[t] for t in range(8)]
    ranks = []
    for t in range(8):
        rank = jnp.int32(0)
        for u in range(t):
            rank = rank + (seqs[u] == seqs[t]).astype(jnp.int32)
        ranks.append(rank)
    place = [seqs[t] * STEPS + ranks[t] for t in range(8)]
    idx = []
    for g in range(8):
        at = jnp.int32(0)
        for t in range(8):
            at = at + t * (place[t] == g).astype(jnp.int32)
        idx.append(at)

    pi = lax.broadcasted_iota(jnp.int32, (ROWS, 128), 0)
    pj = lax.broadcasted_iota(jnp.int32, (ROWS, 128), 1)
    blk = (pi >> 4) & 15
    owner = jnp.where(pi < 256, cs[1], cs[0])
    for b, (dx, dy) in enumerate(XY_FAR):
        owner = owner + jnp.where(blk == b, xs[dx] + ys[dy], 0)
    want = ((pi >> 2) & 3) * 128 + owner * 4 + (pi & 3)
    perm = jnp.concatenate([jnp.where(pj + 128 * r == want, 1.0, 0.0).astype(BF) for r in range(STEPS)], axis=1)
    loads[0].wait()

    def sort_q(s):
        qt = jnp.concatenate([qv[idx[s * STEPS + r]] for r in range(STEPS)], axis=1)
        qss[s][...] = lax.dot_general(perm, qt, NT, preferred_element_type=F32).astype(BF)

    starts = [len_ref[s] - me * CTX for s in range(2)]

    def qk(s, j):
        kcopy(s, j).wait()
        r = jnp.dot(qss[s][...], kvs[s][:, j * KC:(j + 1) * KC], preferred_element_type=F32)
        pos = lax.broadcasted_iota(jnp.int32, (1, KC), 1) + j * KC
        r = jnp.where(pos < starts[s], r * C2, NEG)
        scs[s][:, j * KC:(j + 1) * KC] = r
        mx = r[:, :128]
        for c in range(1, KC // 128):
            mx = jnp.maximum(mx, r[:, c * 128:(c + 1) * 128])
        mrun[s] = mx if j == 0 else jnp.maximum(mrun[s], mx)

    def fin(s):
        m = jnp.max(mrun[s], axis=1, keepdims=True)
        m = jnp.maximum(m, FLOOR).astype(BF).astype(F32)
        m2[s] = jnp.broadcast_to(m, (ROWS, 128))

    def pv(s, j, lo, hi):
        for rb in range(lo // RB, hi // RB):
            rows = slice(rb * RB, (rb + 1) * RB)
            mm = m2[s, rows, :]
            l = jnp.zeros((RB, 128), F32) if j == 0 else lrun[s, rows, :]
            for c in range(KP // 128):
                p = jnp.exp2(scs[s][rows, j * KP + c * 128:j * KP + (c + 1) * 128] - mm)
                l = l + p
                pbs[j % 2][rows, c * 128:(c + 1) * 128] = p.astype(BF)
            lrun[s, rows, :] = l
        r = lax.dot_general(
            pbs[j % 2][lo:hi, :], kvs[s][:LAT, j * KP:(j + 1) * KP], NT, preferred_element_type=F32
        )
        if j == 0:
            accs[s][lo:hi, :] = r
        else:
            accs[s][lo:hi, :] += r

    def landed(buf, sem, n):
        view = buf.at[pl.ds(0, n)]
        pltpu.make_async_copy(view, view, sem).wait()

    def pack(buf, acc, m, l):
        lane = lax.broadcasted_iota(jnp.int32, m.shape, 1)
        l_hi = l.astype(BF).astype(F32)
        ext = jnp.where(lane < 32, m, jnp.where(lane < 64, l_hi, l - l_hi))
        buf[:, :, 0:LAT] = acc.astype(BF).reshape(-1, 16, LAT)
        buf[:, :, LAT:MW] = ext.astype(BF).reshape(-1, 16, 128)

    def total(s, rows):
        return jnp.sum(lrun[s, rows, :], axis=1, keepdims=True)

    def to_sibling(s):
        rows = slice(0, 256)
        pack(send_s.at[s], accs[s][rows, :], m2[s, rows, :], total(s, rows))
        pltpu.make_async_remote_copy(
            send_s.at[s], recv_s.at[s], ssem.at[8], rsem.at[9 + s], device_id=(xs[0] + ys[0] + cs[1], my_dp),
            device_id_type=pl.DeviceIdType.MESH,
        ).start()

    def to_owners(s, lo, hi):
        rows = slice(256 + lo * 16, 256 + hi * 16)
        m_a = m2[s, rows, :]
        ext = recv_s[s, lo:hi, :, LAT:MW].astype(F32).reshape(-1, 128)
        m_b = ext[:, 0:1]
        l_b = ext[:, 32:33] + ext[:, 64:65]
        top = jnp.maximum(m_a, m_b)
        w_a = jnp.exp2(m_a - top)
        w_b = jnp.exp2(m_b - top)
        acc = accs[s][rows, :] * w_a[:, 0:1] + recv_s[s, lo:hi, :, 0:LAT].astype(F32).reshape(-1, LAT) * w_b[:, 0:1]
        pack(send_a.at[s, lo:hi], acc, top, total(s, rows) * w_a + l_b * w_b)
        for b in range(lo, min(hi, 15)):
            dx, dy = XY_FAR[b]
            pltpu.make_async_remote_copy(
                send_a.at[s, b], recv_a.at[s, b], ssem.at[0], rsem.at[s], device_id=(xs[dx] + ys[dy] + cs[0], my_dp),
                device_id_type=pl.DeviceIdType.MESH,
            ).start()
        if hi == 16:
            recv_a[s, 15] = send_a[s, 15]

    sort_q(0)
    for j in range(NCH):
        qk(0, j)
    fin(0)
    sort_q(1)
    for j in range(NPV):
        qk(1, j)
        pv(0, j, 0, ROWS)
    pl.semaphore_wait(barrier, N_KV - 1 + N_DP - 1)
    to_sibling(0)
    qk(1, 2)
    qk(1, 3)
    landed(recv_s.at[0], rsem.at[9], 16)
    to_owners(0, 0, 16)
    fin(1)
    for j in range(NPV):
        pv(1, j, 0, 256)
    to_sibling(1)
    for j in range(NPV):
        pv(1, j, 256, 384)
    landed(recv_s.at[1], rsem.at[10], 16)
    to_owners(1, 0, 8)
    for j in range(NPV):
        pv(1, j, 384, 512)
    to_owners(1, 8, 16)

    loads[5].wait()
    loads[6].wait()
    wgt[...] = wg[...].T
    wut[...] = wu[...].T

    loads[1].wait()
    drafts = drv[...].astype(F32)
    poss = [pos_ref[t] for t in range(8)]
    posg = [pos_ref[idx[g]] for g in range(8)]
    d_score, d_max = [], []
    rowi = lax.broadcasted_iota(jnp.int32, (16, 1), 0) >> 2
    for s in range(2):
        q_own = qss[s][496:512, :].astype(F32)
        my_pos = jnp.zeros((16, 1), jnp.int32)
        for r in range(STEPS):
            my_pos = jnp.where(rowi == r, posg[s * STEPS + r], my_pos)
        cols = []
        for t in range(8):
            sct = jnp.sum(q_own * drafts[t:t + 1, :], axis=1, keepdims=True) * C2
            limit = jnp.where(seqs[t] == s, poss[t], jnp.int32(2 ** 30))
            cols.append(jnp.where(my_pos >= limit, sct, NEG))
        d_score.append(cols)
        d_max.append(functools.reduce(jnp.maximum, cols))

    lats = []
    for s in range(2):
        landed(recv_a.at[s], rsem.at[s], 15)
        ext = recv_a[s, :, :, LAT:MW].astype(F32)
        m_k = ext[:, :, 0:1]
        l_k = ext[:, :, 32:33] + ext[:, :, 64:65]
        top = jnp.maximum(jnp.max(m_k, axis=0), d_max[s])
        w_k = jnp.exp2(m_k - top[None])
        den = jnp.sum(w_k * l_k, axis=0)
        num = jnp.zeros((16, LAT), F32)
        for k in range(16):
            num = num + w_k[k] * recv_a[s, k, :, 0:LAT].astype(F32)
        for t in range(8):
            p = jnp.exp2(d_score[s][t] - top)
            den = den + p
            num = num + p.astype(BF).astype(F32) * drafts[t:t + 1, :LAT]
        lats.append((num / den).astype(BF))
    lat = jnp.concatenate(lats, axis=0)

    loads[2].wait()
    hrow = lax.broadcasted_iota(jnp.int32, (32, 1), 0) & 3
    vals = jnp.concatenate(
        [jnp.where(hrow == h, jnp.dot(lat, wuv[h], preferred_element_type=F32), 0.0) for h in range(4)], axis=1
    ).astype(BF)
    ut = lax.broadcasted_iota(jnp.int32, (8, 32), 0)
    uc = lax.broadcasted_iota(jnp.int32, (8, 32), 1) >> 2
    want_at = jnp.zeros((8, 32), jnp.int32)
    for t in range(8):
        want_at = jnp.where(ut == t, place[t], want_at)
    unsort = jnp.where(uc == want_at, 1.0, 0.0).astype(BF)
    v8 = jnp.dot(unsort, vals, preferred_element_type=F32)
    send_b[...] = jnp.concatenate([v8[:, :256], v8[:, 256:]], axis=0).astype(BF)
    recv_b[my_dp] = send_b[...]

    def over_dp(src, dst, s_sem, r_sem):
        for dz in Z_FAR:
            to = lax.rem(my_dp + dz, N_DP)
            pltpu.make_async_remote_copy(
                src(to), dst.at[my_dp], s_sem, r_sem, device_id=(me, to), device_id_type=pl.DeviceIdType.MESH
            ).start()

    def scatter_kv(src, dst, s_sem, r_sem):
        for dx, dy, dc in KV_FAR:
            to = xs[dx] + ys[dy] + cs[dc]

            @pl.when(to < N_TILE)
            def _():
                pltpu.make_async_remote_copy(
                    src.at[to], dst.at[me], s_sem, r_sem, device_id=(to, my_dp), device_id_type=pl.DeviceIdType.MESH
                ).start()

    def gather_kv(src, dst, s_sem, r_sem):
        for dx, dy, dc in KV_FAR:
            to = xs[dx] + ys[dy] + cs[dc]
            pltpu.make_async_remote_copy(
                src, dst, s_sem, r_sem, device_id=(to, my_dp), device_id_type=pl.DeviceIdType.MESH
            ).start()

    def tiles(x, buf):
        xb = x.astype(BF)
        for rc in range(4):
            for ct in range(7):
                buf[rc * 7 + ct] = xb[rc * 16:(rc + 1) * 16, ct * 128:(ct + 1) * 128]

    def whole(buf):
        return jnp.concatenate(
            [jnp.concatenate([buf[rc * 7 + ct].astype(F32) for ct in range(7)], axis=1) for rc in range(4)], axis=0
        )

    over_dp(lambda to: send_b, recv_b, ssem.at[1], rsem.at[2])
    landed(recv_b, rsem.at[2], N_DP - 1)
    loads[3].wait()
    all_vals = []
    for d in range(N_DP):
        both = recv_b[d].astype(F32)
        all_vals.append(jnp.concatenate([both[:8], both[8:]], axis=1))
    all_vals = jnp.concatenate(all_vals, axis=0).astype(BF)
    tiles(jnp.dot(all_vals, wout[...], preferred_element_type=F32), send_c)
    scatter_kv(send_c, recv_c, ssem.at[2], rsem.at[3])
    loads[4].wait()

    @pl.when(me < N_TILE)
    def _():
        recv_c[me] = send_c[me]
        landed(recv_c, rsem.at[3], N_KV - 1)
        total = jnp.sum(recv_c[...].astype(F32), axis=0)
        rc, ct = lax.div(me, 7), lax.rem(me, 7)
        own = hid[pl.ds(pl.multiple_of(rc * 16, 16), 16), pl.ds(pl.multiple_of(ct * 128, 128), 128)]
        send_d[...] = (own.astype(F32) + total).astype(BF)
        recv_d[me] = send_d[...]
        gather_kv(send_d, recv_d.at[me], ssem.at[3], rsem.at[4])
        landed(recv_d, rsem.at[4], N_TILE - 1)

    @pl.when(me >= N_TILE)
    def _():
        landed(recv_d, rsem.at[4], N_TILE)

    resid = whole(recv_d)
    square = jnp.sum(resid * resid, axis=1, keepdims=True)
    sq_hi = square.astype(BF).astype(F32)
    scaled = (resid * gain_ref[...][None, :]).astype(BF)
    gate = jnp.dot(scaled, wgt[:, :256], preferred_element_type=F32)
    up = jnp.dot(scaled, wut[:, :256], preferred_element_type=F32)
    for d in range(N_DP):
        rows = slice(d * 8, (d + 1) * 8)
        send_e[d] = jnp.concatenate([gate[rows], up[rows]], axis=0).astype(BF)
    over_dp(lambda to: send_e.at[to], recv_e, ssem.at[4], rsem.at[5])
    gate = jnp.dot(scaled, wgt[:, 256:], preferred_element_type=F32)
    up = jnp.dot(scaled, wut[:, 256:], preferred_element_type=F32)
    gate = jnp.concatenate([gate, jnp.broadcast_to(sq_hi, (64, MW - FF_DEV))], axis=1)
    up = jnp.concatenate([up, jnp.broadcast_to(square - sq_hi, (64, MW - FF_DEV))], axis=1)
    for d in range(N_DP):
        rows = slice(d * 8, (d + 1) * 8)
        send_x[d] = jnp.concatenate([gate[rows], up[rows]], axis=0).astype(BF)
    over_dp(lambda to: send_x.at[to], recv_x, ssem.at[9], rsem.at[11])
    recv_e[my_dp] = send_e[my_dp]
    recv_x[my_dp] = send_x[my_dp]
    landed(recv_e, rsem.at[5], N_DP - 1)
    left = jnp.sum(recv_e[...].astype(F32), axis=0)
    landed(recv_x, rsem.at[11], N_DP - 1)
    right = jnp.sum(recv_x[...].astype(F32), axis=0)
    total = jnp.concatenate([left, right], axis=1)
    sq = total[0:8, FF_DEV:FF_DEV + 1] + total[8:16, FF_DEV:FF_DEV + 1]
    inv = lax.rsqrt(sq / D + 1e-06)
    g = total[0:8, :FF_DEV] * inv
    u = total[8:16, :FF_DEV] * inv
    act = g / (1.0 + jnp.exp(-g)) * u
    right = jnp.concatenate([act[:, 384:], jnp.zeros((8, 192), F32)], axis=1)
    send_f[...] = jnp.concatenate([act[:, :384], right], axis=0).astype(BF)
    recv_f[my_dp] = send_f[...]
    over_dp(lambda to: send_f, recv_f, ssem.at[5], rsem.at[6])
    landed(recv_f, rsem.at[6], N_DP - 1)
    acts = []
    for d in range(N_DP):
        both = recv_f[d].astype(F32)
        acts.append(jnp.concatenate([both[:8], both[8:, :192]], axis=1))
    acts = jnp.concatenate(acts, axis=0).astype(BF)
    loads[7].wait()
    tiles(jnp.dot(acts, wd[...], preferred_element_type=F32), send_g)
    scatter_kv(send_g, recv_g, ssem.at[6], rsem.at[7])

    @pl.when(me < N_TILE)
    def _():
        recv_g[me] = send_g[me]
        landed(recv_g, rsem.at[7], N_KV - 1)
        total = jnp.sum(recv_g[...].astype(F32), axis=0)
        done = send_d[...].astype(F32) + total
        send_h[...] = done.astype(BF)
        spot = out_ref.at[lax.rem(me, 7), pl.ds(pl.multiple_of(lax.div(me, 7) * 16, 16), 16)]
        gather_kv(send_h, spot, ssem.at[7], rsem.at[8])
        mine = pltpu.make_async_copy(send_h, spot, lsem.at[8])
        mine.start()
        mine.wait()
        landed(count_h, rsem.at[8], N_TILE - 1)

    @pl.when(me >= N_TILE)
    def _():
        landed(count_h, rsem.at[8], N_TILE)


    for s in range(2):
        landed(send_a.at[s], ssem.at[0], 15)
        landed(send_s.at[s], ssem.at[8], 16)
    landed(recv_b, ssem.at[1], N_DP - 1)
    landed(recv_e, ssem.at[4], N_DP - 1)
    landed(recv_x, ssem.at[9], N_DP - 1)
    landed(recv_f, ssem.at[5], N_DP - 1)

    @pl.when(me < N_TILE)
    def _():
        landed(send_c, ssem.at[2], N_TILE - 1)
        landed(send_g, ssem.at[6], N_TILE - 1)
        landed(recv_c, ssem.at[3], N_KV - 1)
        landed(count_h, ssem.at[7], N_KV - 1)

    @pl.when(me >= N_TILE)
    def _():
        landed(send_c, ssem.at[2], N_TILE)
        landed(send_g, ssem.at[6], N_TILE)


def on_device(queries, drafts, cache, lengths, row_seq, row_pos, w_uv, w_out, hidden, gain, w_gate, w_up, w_down):
    smem = pl.BlockSpec(memory_space=pltpu.SMEM)
    vmem = pl.BlockSpec(memory_space=pltpu.VMEM)
    hbm = pl.BlockSpec(memory_space=pl.ANY)
    v = pltpu.VMEM
    scratch = [
        v((8, W, 128), BF), v((ROWS, W), BF), v((ROWS, W), BF), v((W, CTX), BF), v((W, CTX), BF),
        v((ROWS, CTX), F32), v((ROWS, CTX), F32), v((ROWS, KP), BF), v((ROWS, KP), BF),
        v((2, ROWS, 128), F32), v((2, ROWS, 128), F32), v((2, ROWS, 128), F32), v((ROWS, LAT), F32), v((ROWS, LAT), F32),
        v((8, W), BF), v((4, LAT, HD), BF), v((4 * HD, DC), BF), v((64, DC), BF), v((FF_DEV, DC), BF), v((FF_DEV, DC), BF), v((FF_DEV, DC), BF), v((DC, FF_DEV), BF), v((DC, FF_DEV), BF),
        v((2, 16, 16, MW), BF), v((2, 16, 16, MW), BF), v((2, 16, 16, MW), BF), v((2, 16, 16, MW), BF),
        v((16, 256), BF), v((N_DP, 16, 256), BF),
        v((N_TILE, 16, 128), BF), v((N_KV, 16, 128), BF),
        v((16, 128), BF), v((N_TILE, 16, 128), BF),
        v((N_DP, 16, 256), BF), v((N_DP, 16, 256), BF), v((N_DP, 16, 384), BF), v((N_DP, 16, 384), BF),
        v((16, 384), BF), v((N_DP, 16, 384), BF),
        v((N_TILE, 16, 128), BF), v((N_KV, 16, 128), BF),
        v((16, 128), BF), v((N_KV, 16, 128), BF),
        pltpu.SemaphoreType.DMA((2, NCH)), pltpu.SemaphoreType.DMA((9,)), pltpu.SemaphoreType.DMA((10,)), pltpu.SemaphoreType.DMA((12,)),
    ]
    out = pl.pallas_call(
        kernel,
        out_shape=jax.ShapeDtypeStruct((7, 64, 128), BF),
        in_specs=[smem] * 3 + [hbm] * 6 + [vmem] + [hbm] * 3,
        out_specs=hbm,
        scratch_shapes=scratch,
        compiler_params=pltpu.CompilerParams(
            collective_id=0, has_side_effects=True, vmem_limit_bytes=60 << 20
        ),
        name="verify_layer",
    )(
        lengths, row_seq, row_pos, jnp.swapaxes(queries, 1, 2), drafts, jnp.swapaxes(cache, 1, 2), w_uv, w_out, hidden,
        gain, w_gate.T, w_up.T, w_down,
    )
    return out.swapaxes(0, 1).reshape(64, DC)


def solution(mesh):
    placed = (
        P("dp", None, None),
        P("dp", None),
        P("dp", "kv", None),
        P("dp"),
        P("dp"),
        P("dp"),
        P("kv", None, None),
        P("kv", "dp"),
        P(None, "dp"),
        P("dp"),
        P("dp", "kv"),
        P("dp", "kv"),
        P("kv", "dp"),
    )
    return jax.shard_map(
        on_device, mesh=mesh, in_specs=placed, out_specs=P(None, "dp"), check_vma=False
    )
```
